32 devices in a mesh: dp: 16 (over z, y, core), tensor: 2 (over x).
Axes of the slice: x: 2, y: 2, z: 4, core: 2. Of those that a mesh axis runs over, the one named last changes fastest.
Arguments:
- tokens: bfloat16 [6144, 4096], P(('dp', 'tensor')), may hold values from -21 to 21
- wq_codes: bfloat16 [4096, 1024], P('dp', 'tensor'), may hold values from -4 to 4
- wq_scales: float32 [32, 8], replicated, may hold values from 0.0078125 to 0.03125
- wk_codes: bfloat16 [4096, 128], P('dp', 'tensor'), may hold values from -4 to 4
- wk_scales: float32 [32, 1], replicated, may hold values from 0.0078125 to 0.03125
- wv_codes: bfloat16 [4096, 128], P('dp', 'tensor'), may hold values from -4 to 4
- wv_scales: float32 [32, 1], replicated, may hold values from 0.0078125 to 0.03125
- wo_codes: bfloat16 [1024, 4096], P('tensor', 'dp'), may hold values from -4 to 4
- wo_scales: float32 [8, 32], replicated, may hold values from 0.015625 to 0.0625
Outputs:
- mixed: bfloat16 [6144, 4096], P(('dp', 'tensor'))
The draws below stay inside these ranges and needn't reach their ends.
All inputs are finite; a program needn't handle non-finite values.
Results may differ from the reference program's by a relative error of at most 0.014.
The reference program's roundings to bfloat16 on the way count: a program that leaves them out, or rounds other values in their place, can miss the bound.
Values may be sent and summed in bfloat16 or wider, within the bound.
A program may use at most 64 MiB of HBM per device.

```python
import math
import jax
import jax.numpy as jnp
from jax import lax

D = 4096
HEAD = 128
QH_DEV = 4
GROUP = 8
BLOCK = 128
SPAN = 384
Q_HEADS = 8
KV_HEADS = 1
QW = 1024
KVW = 128
TOKENS = 6144
N_TENSOR = 2


def draw_tokens(key, part):
    base_key = jax.random.fold_in(jax.random.fold_in(key, 11), 0)
    return jax.random.truncated_normal(base_key, -4.0, 4.0, (TOKENS, D), jnp.float32).astype(jnp.bfloat16)


def shard_levels(rng, extent, shards, smallest, largest):
    gain = 1.0
    for axis_at, blocks in shards:
        heights = jax.random.uniform(jax.random.fold_in(jax.random.fold_in(rng, 6), axis_at), (blocks,), jnp.float32, smallest / len(shards), largest / len(shards))
        gain = gain * jnp.repeat(jnp.exp(heights), extent[axis_at] // blocks).reshape((-1,) + (1,) * (len(extent) - 1 - axis_at))
    return gain


def centred(key, extent, scale, most, shards=(), dtype=jnp.bfloat16):
    gain = shard_levels(key, extent, shards, -0.22, 0.18) if shards else 1.0
    entries = jax.random.normal(key, extent, jnp.float32) * scale * gain
    return jnp.minimum(jnp.maximum(entries, -most), most).astype(dtype)


def setup_inputs(seed: int = 0) -> dict:
    key_list = jax.random.split(jax.random.key(seed), 10)
    return {
        "tokens": draw_tokens(jax.random.fold_in(key_list[9], 71), 0),
        "wq_codes": centred(key_list[1], (D, QW), 1.0, 4.0, ((0, 16), (1, 2))),
        "wq_scales": jnp.clip(jnp.exp(jax.random.uniform(key_list[2], (D // BLOCK, QW // BLOCK), jnp.float32, math.log(0.0078125), math.log(0.03125))), 0.0078125, 0.03125),
        "wk_codes": centred(key_list[3], (D, KVW), 1.0, 4.0, ((0, 16), (1, 2))),
        "wk_scales": jnp.clip(jnp.exp(jax.random.uniform(key_list[4], (D // BLOCK, KVW // BLOCK), jnp.float32, math.log(0.0078125), math.log(0.03125))), 0.0078125, 0.03125),
        "wv_codes": centred(key_list[5], (D, KVW), 1.0, 4.0, ((0, 16), (1, 2))),
        "wv_scales": jnp.clip(jnp.exp(jax.random.uniform(key_list[6], (D // BLOCK, KVW // BLOCK), jnp.float32, math.log(0.0078125), math.log(0.03125))), 0.0078125, 0.03125),
        "wo_codes": centred(key_list[7], (QW, D), 1.0, 4.0, ((0, 2), (1, 16))),
        "wo_scales": jnp.clip(jnp.exp(jax.random.uniform(key_list[8], (QW // BLOCK, D // BLOCK), jnp.float32, math.log(0.015625), math.log(0.0625))), 0.015625, 0.0625),
    }


rope_base = 500000.0
masked_value = -1.0e30


def dequantize(codes, scales):
    expanded = jnp.repeat(jnp.repeat(scales, BLOCK, axis=0), BLOCK, axis=1)
    return (codes.astype(jnp.float32) * expanded).astype(jnp.bfloat16)


def rotate(features, positions):
    half_size = HEAD // 2
    steps = jnp.arange(half_size).astype(jnp.float32)
    inverse = jnp.exp(-(2.0 * steps / HEAD) * jnp.log(jnp.float32(rope_base)))
    angle = positions[:, None] * inverse[None, :]
    cosine = jnp.cos(angle)[:, None, :]
    sine = jnp.sin(angle)[:, None, :]
    first = features[..., :half_size]
    second = features[..., half_size:]
    return jnp.concatenate([first * cosine - second * sine, second * cosine + first * sine], axis=-1)


def widen(array):
    return lax.optimization_barrier(array).astype(jnp.float32)


def reference(tokens, wq_codes, wq_scales, wk_codes, wk_scales, wv_codes, wv_scales, wo_codes, wo_scales):
    weight_q = dequantize(wq_codes, wq_scales)
    weight_k = dequantize(wk_codes, wk_scales)
    weight_v = dequantize(wv_codes, wv_scales)
    weight_o = dequantize(wo_codes, wo_scales)
    positions = (jnp.arange(TOKENS) % SPAN).astype(jnp.float32)
    query_lin = jnp.dot(tokens, weight_q, preferred_element_type=jnp.float32).reshape(TOKENS, Q_HEADS, HEAD)
    queries = rotate(query_lin, positions).astype(jnp.bfloat16)
    key_lin = jnp.dot(tokens, weight_k, preferred_element_type=jnp.float32).reshape(TOKENS, KV_HEADS, HEAD)
    keys = rotate(key_lin, positions).astype(jnp.bfloat16)
    values = jnp.dot(tokens, weight_v, preferred_element_type=jnp.float32).astype(jnp.bfloat16).reshape(TOKENS, KV_HEADS, HEAD)
    causal = jnp.arange(SPAN)[:, None] >= jnp.arange(SPAN)[None, :]
    factor = 1.0 / (HEAD ** 0.5)
    span_count = TOKENS // SPAN

    def attend(block):
        span_q, span_k, span_v = block
        wide_k = jnp.repeat(widen(span_k), GROUP, axis=1)
        wide_v = jnp.repeat(widen(span_v), GROUP, axis=1)
        scores = jnp.einsum("qhd,khd->hqk", widen(span_q), wide_k) * factor
        scores = jnp.where(causal[None, :, :], scores, masked_value)
        peak = jnp.max(scores, axis=-1, keepdims=True)
        powers = jnp.exp(scores - peak)
        total = jnp.sum(powers, axis=-1, keepdims=True)
        probs = (powers / total).astype(jnp.bfloat16)
        output = jnp.einsum("hqk,khd->qhd", widen(probs), wide_v)
        return output.astype(jnp.bfloat16).reshape(SPAN, QW)

    attended = lax.map(attend, (queries.reshape(span_count, SPAN, Q_HEADS, HEAD), keys.reshape(span_count, SPAN, KV_HEADS, HEAD), values.reshape(span_count, SPAN, KV_HEADS, HEAD))).reshape(TOKENS, QW)
    group_width = QH_DEV * HEAD
    mixed = jnp.zeros((TOKENS, D), jnp.float32)
    for group in range(N_TENSOR):
        partial_sum = jnp.dot(attended[:, group * group_width:(group + 1) * group_width], weight_o[group * group_width:(group + 1) * group_width], preferred_element_type=jnp.float32)
        mixed = mixed + widen(partial_sum.astype(jnp.bfloat16))
    return mixed.astype(jnp.bfloat16)
```

```python
import jax
import jax.numpy as jnp
import numpy as np
from jax import lax
from jax.experimental import pallas as pl
from jax.experimental.pallas import tpu as pltpu
from jax.sharding import PartitionSpec as P

HEAD = 128
BLOCK = 128
SPAN = 384


rope_base = 500000.0
masked_value = -1e30


def from_partner(value, axis, apart):
    mask = 2**apart
    pairs = [(source, source ^ mask) for source in range(lax.axis_size(axis))]
    return lax.ppermute(value, axis, pairs)


def dequantize(codes, scales, row_start, col_start):
    height, breadth = codes.shape
    row_block = (row_start + jnp.arange(height, dtype=jnp.int32)) // BLOCK
    col_block = (col_start + jnp.arange(breadth, dtype=jnp.int32)) // BLOCK
    row_pick = (row_block[:, None] == jnp.arange(scales.shape[0], dtype=jnp.int32)[None, :]).astype(
        jnp.float32
    )
    col_pick = (col_block[None, :] == jnp.arange(scales.shape[1], dtype=jnp.int32)[:, None]).astype(
        jnp.float32
    )
    picked = jnp.dot(row_pick, scales, precision=lax.Precision.HIGHEST)
    expanded = jnp.dot(picked, col_pick, precision=lax.Precision.HIGHEST)
    return (codes.astype(jnp.float32) * expanded).astype(jnp.bfloat16)


def rotate(features, positions):
    half_size = HEAD // 2
    steps = jnp.arange(half_size).astype(jnp.float32)
    inverse = jnp.exp(-(2.0 * steps / HEAD) * jnp.log(jnp.float32(rope_base)))
    angle = positions[:, None] * inverse[None, :]
    cosine = jnp.cos(angle)[:, None, :]
    sine = jnp.sin(angle)[:, None, :]
    first = features[..., :half_size]
    second = features[..., half_size:]
    return jnp.concatenate(
        [first * cosine - second * sine, second * cosine + first * sine], axis=-1
    )


def in_order(upper, mine, partner):
    return jnp.where(
        upper, jnp.concatenate([partner, mine], axis=1), jnp.concatenate([mine, partner], axis=1)
    )


def body(
    tokens, wq_codes, wq_scales, wk_codes, wk_scales, wv_codes, wv_scales, wo_codes, wo_scales
):
    data_index = lax.axis_index("dp")
    head_index = lax.axis_index("tensor")
    weight_rows = wq_codes.shape[0]
    row_start = data_index * weight_rows
    query_width = wq_codes.shape[1]
    shard_width = wk_codes.shape[1]
    wq_local = dequantize(wq_codes, wq_scales, row_start, head_index * query_width)
    wk_local = dequantize(wk_codes, wk_scales, row_start, head_index * shard_width)
    wv_local = dequantize(wv_codes, wv_scales, row_start, head_index * shard_width)
    wo_local = dequantize(
        wo_codes, wo_scales, head_index * wo_codes.shape[0], data_index * wo_codes.shape[1]
    )
    wo_whole = lax.all_gather(wo_local, "dp", axis=1, tiled=True)
    sequence = lax.all_gather(tokens, "tensor", axis=0, tiled=True)
    upper = head_index % 2 == 1
    partner_k, partner_v = from_partner((wk_local, wv_local), "tensor", 0)
    wk_used = in_order(upper, wk_local, partner_k)
    wv_used = in_order(upper, wv_local, partner_v)
    length = sequence.shape[0]
    full_q, full_k, full_v = (
        lax.all_gather(wq_local, "dp", axis=0, tiled=True),
        lax.all_gather(wk_used, "dp", axis=0, tiled=True),
        lax.all_gather(wv_used, "dp", axis=0, tiled=True),
    )
    query_lin = jnp.dot(sequence, full_q, preferred_element_type=jnp.float32)
    key_lin = jnp.dot(sequence, full_k, preferred_element_type=jnp.float32)
    value_lin = jnp.dot(sequence, full_v, preferred_element_type=jnp.float32)
    positions = (jnp.arange(length) % SPAN).astype(jnp.float32)
    heads_here = query_width // HEAD
    span_count = length // SPAN
    queries = rotate(query_lin.reshape(length, heads_here, HEAD), positions).astype(jnp.bfloat16)
    keys = rotate(key_lin.reshape(length, 1, HEAD), positions)[:, 0, :].astype(jnp.bfloat16)
    values = value_lin.astype(jnp.bfloat16)
    queries = queries.reshape(span_count, SPAN, heads_here, HEAD)
    keys = keys.reshape(span_count, SPAN, HEAD)
    values = values.reshape(span_count, SPAN, HEAD)
    causal = jnp.arange(SPAN)[:, None] >= jnp.arange(SPAN)[None, :]
    scores = jnp.einsum("cqhd,ckd->chqk", queries, keys, preferred_element_type=jnp.float32) * (
        1.0 / HEAD**0.5
    )
    scores = jnp.where(causal[None, None, :, :], scores, masked_value)
    peak = jnp.max(scores, axis=-1, keepdims=True)
    powers = jnp.exp(scores - peak)
    total = jnp.sum(powers, axis=-1, keepdims=True)
    probs = (powers / total).astype(jnp.bfloat16)
    attended = (
        jnp.einsum("chqk,ckd->cqhd", probs, values, preferred_element_type=jnp.float32)
        .astype(jnp.bfloat16)
        .reshape(length, query_width)
    )
    terms = jnp.dot(attended, wo_whole, preferred_element_type=jnp.float32)
    mixed = lax.psum_scatter(terms.astype(jnp.bfloat16), "tensor", scatter_dimension=0, tiled=True)
    return mixed


MESH = pl.DeviceIdType.MESH
Z, Y, CORES = 4, 2, 2
ROWS = 192
DEPTH = 256
WIDTH = 512
MODEL = 4096
TOKEN_PIECES = 4


def rope_tables():
    steps = np.arange(HEAD // 2, dtype=np.float64)
    inverse = rope_base ** (-2.0 * steps / HEAD)
    angle = np.arange(SPAN, dtype=np.float64)[:, None] * inverse[None, :]
    cosine, sine = np.cos(angle), np.sin(angle)
    return (
        np.concatenate([cosine, cosine], axis=1).astype(np.float32),
        np.concatenate([-sine, sine], axis=1).astype(np.float32),
    )


def scaled(codes, scale):
    return (codes.astype(jnp.float32) * scale).astype(jnp.bfloat16)


def fused_kernel(
    tokens, wq, wq_s, wk, wk_s, wv, wv_s, wo, wo_s, cos_ref, sin_ref, out,
    seq, wqkv, wob, kv_pair, acc, q_buf, k_buf, v_buf, att, sent, got, kept,
    z_send, z_recv, y_send, y_recv, c_send, c_recv, t_send, t_recv, t_local, kv_send, kv_recv, o_send, o_recv,
):
    me = lax.axis_index("dp")
    x = lax.axis_index("tensor")
    core = me % CORES
    y = (me // CORES) % Y
    z = me // (CORES * Y)
    across = 1 - x

    def index(zz, yy, cc):
        return (zz * Y + yy) * CORES + cc

    def block(i, cc):
        return index((z - i + 8) % Z, (y + i // 4) % Y, cc)

    y_dev = (index(z, 1 - y, core), x)
    c_dev = (index(z, y, 1 - core), x)
    x_dev = (me, across)
    z_devs = [(index((z + k) % Z, y, core), x) for k in range(1, Z)]

    barrier = pltpu.get_barrier_semaphore()
    for dev in [x_dev, y_dev, c_dev] + z_devs:
        pl.semaphore_signal(barrier, inc=1, device_id=dev, device_id_type=MESH)

    mine_rows = pl.multiple_of(x * ROWS, 16)
    other_rows = pl.multiple_of(across * ROWS, 16)
    local = pltpu.make_async_copy(tokens, seq.at[pl.ds(mine_rows, ROWS), :], t_local)
    local.start()

    def slot(piece, d):
        if piece < 3:
            return wqkv.at[piece, pl.ds(pl.multiple_of(d * DEPTH, DEPTH), DEPTH), :]
        return wob.at[piece - 3, :, pl.ds(pl.multiple_of(d * 128, 128), 128)]

    def remote(ref, send, recv, dev):
        return pltpu.make_async_remote_copy(
            src_ref=ref, dst_ref=ref, send_sem=send, recv_sem=recv, device_id=dev, device_id_type=MESH
        )

    def along_z(piece, k, d):
        return remote(slot(piece, d), z_send.at[piece, k - 1], z_recv.at[piece, k - 1], z_devs[k - 1])

    def along_y(piece, i, d):
        return remote(slot(piece, d), y_send.at[piece, i], y_recv.at[piece, i], y_dev)

    def to_core(piece, i, d):
        return remote(slot(piece, d), c_send.at[piece, i], c_recv.at[piece, i], c_dev)

    sends = []

    def go(copy):
        copy.start()
        sends.append(copy)

    def send_own(piece):
        for k in (2, 1, 3):
            go(along_z(piece, k, me))
        go(along_y(piece, 0, me))
        go(to_core(piece, 0, me))

    def forward_z(piece):
        for k in (1, 3, 2):
            d = block(k, core)
            along_z(piece, k, d).wait_recv()
            go(along_y(piece, k, d))
            go(to_core(piece, k, d))

    def forward_y(piece):
        for i in range(4):
            d = block(4 + i, core)
            along_y(piece, i, d).wait_recv()
            go(to_core(piece, 4 + i, d))

    row0 = me * DEPTH
    for i in range(2):
        rows = pl.ds(i * 128, 128)
        kv_pair[0, rows, :] = jnp.concatenate(
            [scaled(wk[rows, :], wk_s[2 * me + i, 0]), scaled(wv[rows, :], wv_s[2 * me + i, 0])], axis=1
        )
        place = pl.ds(pl.multiple_of(row0 + i * 128, 128), 128)
        for j in range(4):
            wqkv[2 * (j // 2), place, pl.ds((j % 2) * 128, 128)] = scaled(
                wq[rows, pl.ds(j * 128, 128)], wq_s[2 * me + i, 4 * x + j]
            )

    pl.semaphore_wait(barrier, 6)
    kv_copy = pltpu.make_async_remote_copy(
        src_ref=kv_pair.at[0], dst_ref=kv_pair.at[1], send_sem=kv_send, recv_sem=kv_recv,
        device_id=x_dev, device_id_type=MESH,
    )
    go(kv_copy)
    part = ROWS // TOKEN_PIECES
    token_copies = []
    for t in range(TOKEN_PIECES):
        copy = pltpu.make_async_remote_copy(
            src_ref=tokens.at[pl.ds(t * part, part), :],
            dst_ref=seq.at[pl.ds(pl.multiple_of(mine_rows + t * part, 16), part), :],
            send_sem=t_send.at[t], recv_sem=t_recv.at[t], device_id=x_dev, device_id_type=MESH,
        )
        go(copy)
        token_copies.append(copy)
    send_own(0)

    kv_copy.wait_recv()
    own_rows = pl.ds(pl.multiple_of(row0, DEPTH), DEPTH)
    own_kv, far_kv = kv_pair[0], kv_pair[1]
    low = jnp.where(x == 0, own_kv, far_kv)
    high = jnp.where(x == 0, far_kv, own_kv)
    wqkv[1, own_rows, :] = jnp.concatenate([low[:, :64], high[:, :64], low[:, 64:], high[:, 64:]], axis=1)
    send_own(1)
    send_own(2)

    for h in range(2):
        for i in range(4):
            rows = pl.ds(i * 128, 128)
            wob[h, rows, pl.ds(pl.multiple_of(me * 128, 128), 128)] = scaled(
                wo[rows, pl.ds(h * 128, 128)], wo_s[4 * x + i, 2 * me + h]
            )

    forward_z(0)
    forward_z(1)
    forward_y(0)
    forward_z(2)
    send_own(3)
    forward_y(1)
    send_own(4)
    forward_y(2)

    def project(piece):
        for i in range(8):
            to_core(piece, i, block(i, 1 - core)).wait_recv()
        acc[...] = jnp.zeros_like(acc)

        def step(s, carry):
            cut = pl.ds(pl.multiple_of(s * 1024, 1024), 1024)
            acc[...] += jnp.dot(seq[:, cut], wqkv[piece, cut, :], preferred_element_type=jnp.float32)
            return carry

        lax.fori_loop(0, MODEL // 1024, step, 0)

    def roped(cols):
        u = acc[:, cols]
        return (u * cos_ref[...] + pltpu.roll(u, 64, 1) * sin_ref[...]).astype(jnp.bfloat16)

    def attend(h):
        for b in range(3):
            rows = pl.ds(b * 128, 128)
            width = (b + 1) * 128
            scores = lax.dot_general(
                q_buf[h, rows, :], k_buf[pl.ds(0, width), :], (((1,), (1,)), ((), ())),
                preferred_element_type=jnp.float32,
            ) * (1.0 / HEAD**0.5)
            at_row = b * 128 + lax.broadcasted_iota(jnp.int32, (128, width), 0)
            at_col = lax.broadcasted_iota(jnp.int32, (128, width), 1)
            scores = jnp.where(at_row >= at_col, scores, masked_value)
            powers = jnp.exp(scores - jnp.max(scores, axis=-1, keepdims=True))
            total = jnp.sum(powers, axis=-1, keepdims=True)
            probs = (powers / total).astype(jnp.bfloat16)
            att[rows, pl.ds(h * 128, 128)] = jnp.dot(
                probs, v_buf[pl.ds(0, width), :], preferred_element_type=jnp.float32
            ).astype(jnp.bfloat16)

    local.wait()
    for copy in token_copies:
        copy.wait_recv()
    project(0)
    for h in range(2):
        q_buf[h] = roped(slice(h * 128, h * 128 + 128))
    project(1)
    k_buf[...] = roped(slice(0, 128))
    v_buf[...] = acc[:, 128:].astype(jnp.bfloat16)
    attend(0)
    attend(1)
    project(2)
    for h in range(2):
        q_buf[2 + h] = roped(slice(h * 128, h * 128 + 128))
    forward_z(3)
    attend(2)
    attend(3)
    forward_z(4)

    def out_copy(j):
        return pltpu.make_async_remote_copy(
            src_ref=sent.at[j], dst_ref=got.at[j], send_sem=o_send.at[j], recv_sem=o_recv.at[j],
            device_id=x_dev, device_id_type=MESH,
        )

    def chip(i):
        return block(i, 0) // 2

    def produce(h, start):
        def step(i, carry):
            to_core(3 + h, i, block(i, 1 - core)).wait_recv()
            j = h * 8 + i
            w = wob[h, :, pl.ds(pl.multiple_of(chip(i) * 256, 256), 256)]
            sent[j] = jnp.dot(
                att[pl.ds(other_rows, ROWS), :], w, preferred_element_type=jnp.float32
            ).astype(jnp.bfloat16)
            out_copy(j).start()
            kept[j] = jnp.dot(
                att[pl.ds(mine_rows, ROWS), :], w, preferred_element_type=jnp.float32
            ).astype(jnp.bfloat16)
            return carry

        lax.fori_loop(start, start + 4, step, 0)

    produce(0, 0)
    forward_y(3)
    produce(0, 4)
    produce(1, 0)
    forward_y(4)
    produce(1, 4)

    def finish(j, carry):
        h = j // 8
        i = j % 8
        out_copy(j).wait_recv()
        total = (kept[j].astype(jnp.float32) + got[j].astype(jnp.float32)).astype(jnp.bfloat16)
        base = chip(i) * 512 + h * 128
        out[:, pl.ds(pl.multiple_of(base, 128), 128)] = total[:, :128]
        out[:, pl.ds(pl.multiple_of(base + 256, 128), 128)] = total[:, 128:]
        return carry

    lax.fori_loop(0, 16, finish, 0)
    for copy in sends:
        copy.wait_send()

    def drain(j, carry):
        out_copy(j).wait_send()
        return carry

    lax.fori_loop(0, 16, drain, 0)


def fused_body(tokens, wq, wq_s, wk, wk_s, wv, wv_s, wo, wo_s):
    cosine, sine = rope_tables()
    vmem = pl.BlockSpec(memory_space=pltpu.VMEM)
    smem = pl.BlockSpec(memory_space=pltpu.SMEM)
    hbm = pl.BlockSpec(memory_space=pl.ANY)
    dma = pltpu.SemaphoreType.DMA
    bf16 = jnp.bfloat16
    return pl.pallas_call(
        fused_kernel,
        out_shape=jax.ShapeDtypeStruct((ROWS, MODEL), bf16),
        in_specs=[hbm, vmem, smem, vmem, smem, vmem, smem, vmem, smem, vmem, vmem],
        out_specs=vmem,
        scratch_shapes=[
            pltpu.VMEM((SPAN, MODEL), bf16),
            pltpu.VMEM((3, MODEL, 256), bf16),
            pltpu.VMEM((2, WIDTH, MODEL // 2), bf16),
            pltpu.VMEM((2, DEPTH, 128), bf16),
            pltpu.VMEM((SPAN, 256), jnp.float32),
            pltpu.VMEM((4, SPAN, HEAD), bf16),
            pltpu.VMEM((SPAN, HEAD), bf16),
            pltpu.VMEM((SPAN, HEAD), bf16),
            pltpu.VMEM((SPAN, WIDTH), bf16),
            pltpu.VMEM((16, ROWS, 256), bf16),
            pltpu.VMEM((16, ROWS, 256), bf16),
            pltpu.VMEM((16, ROWS, 256), bf16),
            dma((5, 3)), dma((5, 3)), dma((5, 4)), dma((5, 4)), dma((5, 8)), dma((5, 8)),
            dma((TOKEN_PIECES,)), dma((TOKEN_PIECES,)), dma, dma, dma, dma((16,)), dma((16,)),
        ],
        compiler_params=pltpu.CompilerParams(
            collective_id=0, has_side_effects=True, vmem_limit_bytes=48 * 1024 * 1024
        ),
        cost_estimate=pl.CostEstimate(flops=4_500_000_000, bytes_accessed=6_000_000, transcendentals=300_000),
    )(tokens, wq, wq_s, wk, wk_s, wv, wv_s, wo, wo_s, jnp.asarray(cosine), jnp.asarray(sine))


def solution(mesh):

    fits = mesh.shape["dp"] == Z * Y * CORES and mesh.shape["tensor"] == 2
    return jax.shard_map(
        fused_body if fits else body,
        mesh=mesh,
        in_specs=(
            P(("dp", "tensor"), None),
            P("dp", "tensor"),
            P(),
            P("dp", "tensor"),
            P(),
            P("dp", "tensor"),
            P(),
            P("tensor", "dp"),
            P(),
        ),
        out_specs=P(("dp", "tensor"), None),
        check_vma=False,
    )
```

```python
import jax
import jax.numpy as jnp
import numpy as np
from jax import lax
from jax.experimental import pallas as pl
from jax.experimental.pallas import tpu as pltpu
from jax.sharding import PartitionSpec as P

HEAD = 128
BLOCK = 128
SPAN = 384


rope_base = 500000.0
masked_value = -1e30


def from_partner(value, axis, apart):
    mask = 2**apart
    pairs = [(source, source ^ mask) for source in range(lax.axis_size(axis))]
    return lax.ppermute(value, axis, pairs)


def dequantize(codes, scales, row_start, col_start):
    height, breadth = codes.shape
    row_block = (row_start + jnp.arange(height, dtype=jnp.int32)) // BLOCK
    col_block = (col_start + jnp.arange(breadth, dtype=jnp.int32)) // BLOCK
    row_pick = (row_block[:, None] == jnp.arange(scales.shape[0], dtype=jnp.int32)[None, :]).astype(
        jnp.float32
    )
    col_pick = (col_block[None, :] == jnp.arange(scales.shape[1], dtype=jnp.int32)[:, None]).astype(
        jnp.float32
    )
    picked = jnp.dot(row_pick, scales, precision=lax.Precision.HIGHEST)
    expanded = jnp.dot(picked, col_pick, precision=lax.Precision.HIGHEST)
    return (codes.astype(jnp.float32) * expanded).astype(jnp.bfloat16)


def rotate(features, positions):
    half_size = HEAD // 2
    steps = jnp.arange(half_size).astype(jnp.float32)
    inverse = jnp.exp(-(2.0 * steps / HEAD) * jnp.log(jnp.float32(rope_base)))
    angle = positions[:, None] * inverse[None, :]
    cosine = jnp.cos(angle)[:, None, :]
    sine = jnp.sin(angle)[:, None, :]
    first = features[..., :half_size]
    second = features[..., half_size:]
    return jnp.concatenate(
        [first * cosine - second * sine, second * cosine + first * sine], axis=-1
    )


def in_order(upper, mine, partner):
    return jnp.where(
        upper, jnp.concatenate([partner, mine], axis=1), jnp.concatenate([mine, partner], axis=1)
    )


def body(
    tokens, wq_codes, wq_scales, wk_codes, wk_scales, wv_codes, wv_scales, wo_codes, wo_scales
):
    data_index = lax.axis_index("dp")
    head_index = lax.axis_index("tensor")
    weight_rows = wq_codes.shape[0]
    row_start = data_index * weight_rows
    query_width = wq_codes.shape[1]
    shard_width = wk_codes.shape[1]
    wq_local = dequantize(wq_codes, wq_scales, row_start, head_index * query_width)
    wk_local = dequantize(wk_codes, wk_scales, row_start, head_index * shard_width)
    wv_local = dequantize(wv_codes, wv_scales, row_start, head_index * shard_width)
    wo_local = dequantize(
        wo_codes, wo_scales, head_index * wo_codes.shape[0], data_index * wo_codes.shape[1]
    )
    wo_whole = lax.all_gather(wo_local, "dp", axis=1, tiled=True)
    sequence = lax.all_gather(tokens, "tensor", axis=0, tiled=True)
    upper = head_index % 2 == 1
    partner_k, partner_v = from_partner((wk_local, wv_local), "tensor", 0)
    wk_used = in_order(upper, wk_local, partner_k)
    wv_used = in_order(upper, wv_local, partner_v)
    length = sequence.shape[0]
    full_q, full_k, full_v = (
        lax.all_gather(wq_local, "dp", axis=0, tiled=True),
        lax.all_gather(wk_used, "dp", axis=0, tiled=True),
        lax.all_gather(wv_used, "dp", axis=0, tiled=True),
    )
    query_lin = jnp.dot(sequence, full_q, preferred_element_type=jnp.float32)
    key_lin = jnp.dot(sequence, full_k, preferred_element_type=jnp.float32)
    value_lin = jnp.dot(sequence, full_v, preferred_element_type=jnp.float32)
    positions = (jnp.arange(length) % SPAN).astype(jnp.float32)
    heads_here = query_width // HEAD
    span_count = length // SPAN
    queries = rotate(query_lin.reshape(length, heads_here, HEAD), positions).astype(jnp.bfloat16)
    keys = rotate(key_lin.reshape(length, 1, HEAD), positions)[:, 0, :].astype(jnp.bfloat16)
    values = value_lin.astype(jnp.bfloat16)
    queries = queries.reshape(span_count, SPAN, heads_here, HEAD)
    keys = keys.reshape(span_count, SPAN, HEAD)
    values = values.reshape(span_count, SPAN, HEAD)
    causal = jnp.arange(SPAN)[:, None] >= jnp.arange(SPAN)[None, :]
    scores = jnp.einsum("cqhd,ckd->chqk", queries, keys, preferred_element_type=jnp.float32) * (
        1.0 / HEAD**0.5
    )
    scores = jnp.where(causal[None, None, :, :], scores, masked_value)
    peak = jnp.max(scores, axis=-1, keepdims=True)
    powers = jnp.exp(scores - peak)
    total = jnp.sum(powers, axis=-1, keepdims=True)
    probs = (powers / total).astype(jnp.bfloat16)
    attended = (
        jnp.einsum("chqk,ckd->cqhd", probs, values, preferred_element_type=jnp.float32)
        .astype(jnp.bfloat16)
        .reshape(length, query_width)
    )
    terms = jnp.dot(attended, wo_whole, preferred_element_type=jnp.float32)
    mixed = lax.psum_scatter(terms.astype(jnp.bfloat16), "tensor", scatter_dimension=0, tiled=True)
    return mixed


MESH = pl.DeviceIdType.MESH
Z, Y, CORES = 4, 2, 2
ROWS = 192
DEPTH = 256
WIDTH = 512
MODEL = 4096
TOKEN_PIECES = 4
VMEM_BYTES = 62 * 1024 * 1024


def rope_tables():
    steps = np.arange(HEAD // 2, dtype=np.float64)
    inverse = rope_base ** (-2.0 * steps / HEAD)
    angle = np.arange(SPAN, dtype=np.float64)[:, None] * inverse[None, :]
    cosine, sine = np.cos(angle), np.sin(angle)
    return (
        np.concatenate([cosine, cosine], axis=1).astype(np.float32),
        np.concatenate([-sine, sine], axis=1).astype(np.float32),
    )


def scaled(codes, scale):
    return (codes.astype(jnp.float32) * scale).astype(jnp.bfloat16)


def fused_kernel(
    tokens, wq_h, wq_sh, wk_h, wk_sh, wv_h, wv_sh, wo_h, wo_sh, cos_h, sin_h, out,
    wq, wk, wv, wo, cos_ref, sin_ref, wq_s, wk_s, wv_s, wo_s,
    seq, wqkv, wkv, wob, kv_half, kv_far, acc, q_buf, k_buf, v_buf, att, sent, got,
    z_send, z_recv, y_send, y_recv, c_send, c_recv, t_send, t_recv, in_sem, kv_send, kv_recv, o_send, o_recv,
):
    me = lax.axis_index("dp")
    x = lax.axis_index("tensor")
    core = me % CORES
    y = (me // CORES) % Y
    z = me // (CORES * Y)
    across = 1 - x

    def index(zz, yy, cc):
        return (zz * Y + yy) * CORES + cc

    def block(i, cc):
        return index((z - i + 8) % Z, (y + i // 4) % Y, cc)

    y_dev = (index(z, 1 - y, core), x)
    c_dev = (index(z, y, 1 - core), x)
    x_dev = (me, across)
    z_devs = [(index((z + k) % Z, y, core), x) for k in range(1, Z)]

    barrier = pltpu.get_barrier_semaphore()
    for dev in [x_dev, y_dev, c_dev] + z_devs:
        pl.semaphore_signal(barrier, inc=1, device_id=dev, device_id_type=MESH)

    mine_rows = pl.multiple_of(x * ROWS, 64)
    other_rows = pl.multiple_of(across * ROWS, 64)
    pairs = [
        (wk_h, wk), (wv_h, wv), (wk_sh, wk_s), (wv_sh, wv_s), (wq_sh, wq_s), (wq_h, wq),
        (wo_h, wo), (wo_sh, wo_s), (cos_h, cos_ref), (sin_h, sin_ref),
        (tokens, seq.at[pl.ds(mine_rows, ROWS), :]),
    ]
    loads = [pltpu.make_async_copy(a, b, in_sem.at[i]) for i, (a, b) in enumerate(pairs)]
    for load in loads:
        load.start()

    def slot(part, d):
        piece, r = part // 2, part % 2
        if piece == 1:
            return wkv.at[pl.ds(pl.multiple_of(d * DEPTH, DEPTH), DEPTH), :]
        if piece < 3:
            return wqkv.at[piece // 2, pl.ds(pl.multiple_of(d * DEPTH + r * 128, 128), 128), :]
        return wob.at[piece - 3, pl.ds(r * 256, 256), pl.ds(pl.multiple_of(d * 128, 128), 128)]

    def remote(ref, send, recv, dev):
        return pltpu.make_async_remote_copy(
            src_ref=ref, dst_ref=ref, send_sem=send, recv_sem=recv, device_id=dev, device_id_type=MESH
        )

    def along_z(part, d, send, recv, step):
        to = (index((z + step + Z) % Z, y, core), x)
        return remote(slot(part, d), z_send.at[part, send], z_recv.at[part, recv], to)

    def along_y(part, i, d):
        return remote(slot(part, d), y_send.at[part, i], y_recv.at[part, i], y_dev)

    def to_core(part, i, d):
        return remote(slot(part, d), c_send.at[part, i], c_recv.at[part, i], c_dev)

    sends = []

    def go(copy):
        copy.start()
        sends.append(copy)

    maybe = []

    def go_if(condition, copy):
        pl.when(condition)(copy.start)
        maybe.append((condition, copy))

    arrival = [
        jnp.where(z == 0, 3, 1),
        jnp.where((z == 0) | (z == 3), 2, 3),
        jnp.where(z == 0, 1, jnp.where(z == 3, 3, 2)),
    ]

    def own_z(part):
        go_if(z < Z - 1, along_z(part, me, 0, 0, 1))
        go_if(z > 0, along_z(part, me, 1, 2, -1))

    def own_yc(part):
        go(along_y(part, 0, me))
        go(to_core(part, 0, me))

    def forward_z(part):
        for n, i in enumerate(arrival):
            d = block(i, core)
            along_z(part, d, 0, i - 1, 1).wait_recv()
            go_if((i <= z) & (z < Z - 1), along_z(part, d, 2 + n, jnp.minimum(i, 2), 1))
            go_if((i > z) & (z > 0), along_z(part, d, 2 + n, jnp.maximum(i - 2, 0), -1))
            go(along_y(part, i, d))
            go(to_core(part, i, d))

    def forward_y(part):
        for i in range(4):
            d = block(4 + i, core)
            along_y(part, i, d).wait_recv()
            go(to_core(part, 4 + i, d))

    pl.semaphore_wait(barrier, 6)
    part_rows = ROWS // TOKEN_PIECES
    token_copies = []
    for t in range(TOKEN_PIECES):
        copy = pltpu.make_async_remote_copy(
            src_ref=tokens.at[pl.ds(t * part_rows, part_rows), :],
            dst_ref=seq.at[pl.ds(pl.multiple_of(mine_rows + t * part_rows, 16), part_rows), :],
            send_sem=t_send.at[t], recv_sem=t_recv.at[t], device_id=x_dev, device_id_type=MESH,
        )
        go(copy)
        token_copies.append(copy)

    row0 = me * DEPTH

    def scale_q(piece):
        for i in range(2):
            place = pl.ds(pl.multiple_of(row0 + i * 128, 128), 128)
            for j in range(2):
                wqkv[piece // 2, place, pl.ds(j * 128, 128)] = scaled(
                    wq[pl.ds(i * 128, 128), pl.ds(piece * 128 + j * 128, 128)],
                    wq_s[4 * x + piece + j, 2 * me + i],
                )
            own_yc(2 * piece + i)
            if piece == 0:
                own_z(i)

    loads[4].wait()
    loads[5].wait()
    scale_q(0)
    for i in range(4):
        loads[i].wait()
    for i in range(2):
        rows = pl.ds(i * 128, 128)
        both = jnp.concatenate(
            [
                wk[:, rows].astype(jnp.float32) * wk_s[0, 2 * me + i],
                wv[:, rows].astype(jnp.float32) * wv_s[0, 2 * me + i],
            ],
            axis=0,
        )
        wkv[pl.ds(pl.multiple_of(row0 + i * 128, 128), 128), :] = both.T.astype(jnp.bfloat16)
    own_yc(2)
    own_z(2)
    scale_q(2)

    loads[6].wait()
    loads[7].wait()
    for h in range(2):
        for i in range(4):
            rows = pl.ds(i * 128, 128)
            wob[h, rows, pl.ds(pl.multiple_of(me * 128, 128), 128)] = scaled(
                wo[rows, pl.ds(h * 128, 128)], wo_s[4 * x + i, 2 * me + h]
            )
    for i in range(8, 11):
        loads[i].wait()

    def arrived(piece):
        for part in (2,) if piece == 1 else (2 * piece, 2 * piece + 1):
            for i in range(8):
                to_core(part, i, block(i, 1 - core)).wait_recv()

    def project(total, weights, row):
        rows = pl.ds(row, ROWS)
        total[rows, :] = jnp.zeros((ROWS, total.shape[1]), jnp.float32)

        def step(s, carry):
            cut = pl.ds(pl.multiple_of(s * 1024, 1024), 1024)
            total[rows, :] += jnp.dot(seq[rows, cut], weights[cut, :], preferred_element_type=jnp.float32)
            return carry

        lax.fori_loop(0, MODEL // 1024, step, 0)

    def roped(u, row):
        rows = pl.ds(row, ROWS)
        return (u * cos_ref[rows, :] + pltpu.roll(u, 64, 1) * sin_ref[rows, :]).astype(jnp.bfloat16)

    def take_q(piece, row):
        rows = pl.ds(row, ROWS)
        project(acc, wqkv.at[piece // 2], row)
        q_buf[piece, rows, :] = roped(acc[rows, :128], row)
        q_buf[piece + 1, rows, :] = roped(acc[rows, 128:], row)

    def kv_copy(n, row):
        rows = pl.ds(row, ROWS)
        return pltpu.make_async_remote_copy(
            src_ref=kv_half.at[rows, :], dst_ref=kv_far.at[rows, :], send_sem=kv_send.at[n], recv_sem=kv_recv.at[n],
            device_id=x_dev, device_id_type=MESH,
        )

    def take_kv(n, row):
        project(kv_half, wkv, row)
        go(kv_copy(n, row))

    def join_kv(row):
        rows = pl.ds(row, ROWS)
        own_kv, far_kv = kv_half[rows, :], kv_far[rows, :]
        low = jnp.where(x == 0, own_kv, far_kv)
        high = jnp.where(x == 0, far_kv, own_kv)
        k_buf[rows, :] = roped(jnp.concatenate([low[:, :64], high[:, :64]], axis=1), row)
        v_buf[rows, :] = jnp.concatenate([low[:, 64:], high[:, 64:]], axis=1).astype(jnp.bfloat16)

    def attend(h, row):
        rows = pl.ds(row, ROWS)
        scores = lax.dot_general(
            q_buf[h, rows, :], k_buf[...], (((1,), (1,)), ((), ())), preferred_element_type=jnp.float32
        ) * (1.0 / HEAD**0.5)
        at_row = row + lax.broadcasted_iota(jnp.int32, (ROWS, SPAN), 0)
        at_col = lax.broadcasted_iota(jnp.int32, (ROWS, SPAN), 1)
        scores = jnp.where(at_row >= at_col, scores, masked_value)
        powers = jnp.exp(scores - jnp.max(scores, axis=-1, keepdims=True))
        total = jnp.sum(powers, axis=-1, keepdims=True)
        probs = (powers * (1.0 / total)).astype(jnp.bfloat16)
        att[rows, pl.ds(h * 128, 128)] = jnp.dot(
            probs, v_buf[...], preferred_element_type=jnp.float32
        ).astype(jnp.bfloat16)

    forward_z(0)
    own_z(4)
    forward_z(1)
    own_z(5)
    forward_y(0)
    forward_z(2)
    own_z(6)
    own_yc(6)
    forward_y(1)
    forward_z(4)
    own_z(7)
    own_yc(7)
    forward_y(2)
    arrived(0)
    take_q(0, mine_rows)
    forward_z(5)
    own_z(8)
    own_yc(8)
    forward_y(4)
    arrived(1)
    take_kv(0, mine_rows)
    forward_z(6)
    own_z(9)
    own_yc(9)
    forward_z(7)
    forward_y(5)
    forward_z(8)
    for copy in token_copies:
        copy.wait_recv()
    take_kv(1, other_rows)
    take_q(0, other_rows)
    forward_y(6)
    arrived(2)
    take_q(2, other_rows)
    kv_copy(0, other_rows).wait_recv()
    kv_copy(1, mine_rows).wait_recv()
    join_kv(mine_rows)
    join_kv(other_rows)
    for h in range(4):
        attend(h, other_rows)

    def out_copy(j):
        return pltpu.make_async_remote_copy(
            src_ref=sent.at[j], dst_ref=got.at[j], send_sem=o_send.at[j], recv_sem=o_recv.at[j],
            device_id=x_dev, device_id_type=MESH,
        )

    def chip(i):
        return block(i, 0) // 2

    def columns(h, i):
        return wob[h, :, pl.ds(pl.multiple_of(chip(i) * 256, 256), 256)]

    def produce(h, start):
        def step(i, carry):
            for r in range(2):
                to_core(6 + 2 * h + r, i, block(i, 1 - core)).wait_recv()
            j = h * 8 + i
            sent[j] = jnp.dot(
                att[pl.ds(other_rows, ROWS), :], columns(h, i), preferred_element_type=jnp.float32
            ).astype(jnp.bfloat16)
            out_copy(j).start()
            return carry

        lax.fori_loop(start, start + 4, step, 0)

    produce(0, 0)
    forward_z(9)
    forward_y(7)
    produce(0, 4)
    take_q(2, mine_rows)
    forward_y(8)
    produce(1, 0)
    forward_y(9)
    produce(1, 4)
    for h in range(4):
        attend(h, mine_rows)

    def finish(j, carry):
        h = j // 8
        i = j % 8
        kept = jnp.dot(
            att[pl.ds(mine_rows, ROWS), :], columns(h, i), preferred_element_type=jnp.float32
        ).astype(jnp.bfloat16)
        out_copy(j).wait_recv()
        total = (kept.astype(jnp.float32) + got[j].astype(jnp.float32)).astype(jnp.bfloat16)
        base = chip(i) * 512 + h * 128
        out[:, pl.ds(pl.multiple_of(base, 128), 128)] = total[:, :128]
        out[:, pl.ds(pl.multiple_of(base + 256, 128), 128)] = total[:, 128:]
        return carry

    lax.fori_loop(0, 16, finish, 0)
    for copy in sends:
        copy.wait_send()
    for condition, copy in maybe:
        pl.when(condition)(copy.wait_send)

    def drain(j, carry):
        out_copy(j).wait_send()
        return carry

    lax.fori_loop(0, 16, drain, 0)


def fused_body(tokens, wq, wq_s, wk, wk_s, wv, wv_s, wo, wo_s):
    cosine, sine = rope_tables()
    hbm = pl.BlockSpec(memory_space=pl.ANY)
    dma = pltpu.SemaphoreType.DMA
    bf16, f32 = jnp.bfloat16, jnp.float32
    return pl.pallas_call(
        fused_kernel,
        out_shape=jax.ShapeDtypeStruct((ROWS, MODEL), bf16),
        in_specs=[hbm] * 11,
        out_specs=pl.BlockSpec(memory_space=pltpu.VMEM),
        scratch_shapes=[
            pltpu.VMEM((DEPTH, WIDTH), bf16),
            pltpu.VMEM((64, DEPTH), bf16),
            pltpu.VMEM((64, DEPTH), bf16),
            pltpu.VMEM((WIDTH, DEPTH), bf16),
            pltpu.VMEM((SPAN, HEAD), f32),
            pltpu.VMEM((SPAN, HEAD), f32),
            pltpu.SMEM((8, 32), f32),
            pltpu.SMEM((1, 32), f32),
            pltpu.SMEM((1, 32), f32),
            pltpu.SMEM((8, 32), f32),
            pltpu.VMEM((SPAN, MODEL), bf16),
            pltpu.VMEM((2, MODEL, 256), bf16),
            pltpu.VMEM((MODEL, 128), bf16),
            pltpu.VMEM((2, WIDTH, MODEL // 2), bf16),
            pltpu.VMEM((SPAN, HEAD), f32),
            pltpu.VMEM((SPAN, HEAD), f32),
            pltpu.VMEM((SPAN, 256), f32),
            pltpu.VMEM((4, SPAN, HEAD), bf16),
            pltpu.VMEM((SPAN, HEAD), bf16),
            pltpu.VMEM((SPAN, HEAD), bf16),
            pltpu.VMEM((SPAN, WIDTH), bf16),
            pltpu.VMEM((16, ROWS, 256), bf16),
            pltpu.VMEM((16, ROWS, 256), bf16),
            dma((10, 5)), dma((10, 3)), dma((10, 4)), dma((10, 4)), dma((10, 8)), dma((10, 8)),
            dma((TOKEN_PIECES,)), dma((TOKEN_PIECES,)), dma((11,)), dma((2,)), dma((2,)), dma((16,)), dma((16,)),
        ],
        compiler_params=pltpu.CompilerParams(
            collective_id=0, has_side_effects=True, vmem_limit_bytes=VMEM_BYTES
        ),
        cost_estimate=pl.CostEstimate(flops=4_500_000_000, bytes_accessed=6_000_000, transcendentals=300_000),
    )(tokens, wq, wq_s.T, wk.T, wk_s.T, wv.T, wv_s.T, wo, wo_s, jnp.asarray(cosine), jnp.asarray(sine))


def solution(mesh):

    fits = mesh.shape["dp"] == Z * Y * CORES and mesh.shape["tensor"] == 2
    return jax.shard_map(
        fused_body if fits else body,
        mesh=mesh,
        in_specs=(
            P(("dp", "tensor"), None),
            P("dp", "tensor"),
            P(),
            P("dp", "tensor"),
            P(),
            P("dp", "tensor"),
            P(),
            P("tensor", "dp"),
            P(),
        ),
        out_specs=P(("dp", "tensor"), None),
        check_vma=False,
    )
```
